32 devices in a mesh: frames: 2 (over x), date: 16 (over z, y, core).
Axes of the slice: x: 2, y: 2, z: 4, core: 2. Of those that a mesh axis runs over, the one named last changes fastest.
Arguments:
- backward_sensitivity: bfloat16 [512, 2, 256, 256], P(('frames', 'date')), parts along dimension 0, may hold values from -24 to 24
- patch_stack_samples: bfloat16 [512, 2, 256, 128], P(('frames', 'date')), parts along dimension 0, may hold values from -16 to 16
- patch_contribution_factor: float32 [512, 128], P(('frames', 'date')), parts along dimension 0, may hold values from 0.2 to 2
- neighbour_displacements: int32 [512, 128], P(('frames', 'date')), parts along dimension 0, may hold values from 0 to 255, as said below
- delay_quanta: int32 [512], P(('frames', 'date')), parts along dimension 0, may hold values from -256 to 255
- segment_correction_angles: float32 [512, 9], P(('frames', 'date')), parts along dimension 0, may hold values from -3.140625 to 3.140625
- segment_starts: int32 [16], P('frames'), parts along dimension 0, may hold values from 1 to 4095, as said below
Outputs:
- stack_grad: float32 [2, 512, 8, 4096], P(None, ('frames', 'date')), parts along dimension 1
The draws below stay inside these ranges and needn't reach their ends.
There are 2 independent parts, one for each index of `frames`. The reference program is written for one: setup_inputs(seed, part) draws one part's arguments, and reference() takes and returns one part's arrays. A program takes and returns all parts, laid end to end along the dimension named above; each array names one. Nothing has to cross between parts.
Inputs may be any that keep to these rules, and one draw needn't show every extreme that they name: `neighbour_displacements`: the 128 offsets of one window are distinct. `segment_starts`: strictly increasing.
All inputs are finite; a program needn't handle non-finite values.
Results may differ from the reference program's by a relative error of at most 0.0053.
Values may be sent and summed in bfloat16 or wider, within the bound.
A program may use at most 192 MiB of HBM per device.

```python
import math
import jax
import jax.numpy as jnp
from jax import lax

EPOCH_COUNT = 256
ALONG_TRACK_SIZE = 4096
RG = 8
WIN = 128
REACH = 8
QUANT = 16
SEGMENT_COUNT = 9
NWIN = 256
NBHD = 256


def draw_patch_stack_samples(key, part):
    key = jax.random.fold_in(key, 11)
    keys = jax.random.split(key, 5)
    column_scale = jnp.exp(jax.random.uniform(keys[1], (NWIN, 1, 1, WIN), minval=-1.2, maxval=1.2))
    row_scale = jnp.exp(jax.random.uniform(keys[0], (NWIN, 1, EPOCH_COUNT, 1), minval=-1.2, maxval=1.2))
    starting_point = jax.random.normal(keys[4], (NWIN, 2, EPOCH_COUNT, WIN), jnp.float32)
    values = jnp.clip(0.6 * starting_point * row_scale * column_scale, -16.0, 16.0)
    return values.astype(jnp.bfloat16)


def draw_neighbour_displacements(key, part):
    key = jax.random.fold_in(key, 23)
    keys = jax.random.split(key, NWIN)
    picked = jax.vmap(lambda single: jax.random.permutation(single, NBHD)[:WIN])(keys)
    return picked.astype(jnp.int32)


def draw_segment_starts(key, part):
    key = jax.random.fold_in(key, 37)
    stride_gap = ALONG_TRACK_SIZE // (4 * SEGMENT_COUNT)
    starting_point = jnp.arange(1, SEGMENT_COUNT, dtype=jnp.int32) * ALONG_TRACK_SIZE // SEGMENT_COUNT
    random_perturbation = jax.random.randint(key, (SEGMENT_COUNT - 1,), -stride_gap, stride_gap + 1, dtype=jnp.int32)
    return (starting_point + random_perturbation).astype(jnp.int32)


def touch_ends(array, stream_key, least, high):
    dims = array.shape
    spot = [jax.random.randint(jax.random.fold_in(stream_key, axis), (), 0, dims[axis]) for axis in range(len(dims))]
    array = array.at[tuple(spot)].set(least)
    longest = dims.index(max(dims))
    spot[longest] = (spot[longest] + 1) % dims[longest]
    return array.at[tuple(spot)].set(high)


def block_scale(key, extent, cuts, least, top_value):
    factor_of, own = 1.0, jax.random.fold_in(key, 6)
    for axis_at, parts in cuts:
        draws = jnp.exp(jax.random.uniform(jax.random.fold_in(own, axis_at), (parts,), jnp.float32, least / len(cuts), top_value / len(cuts)))
        factor_of = factor_of * jnp.repeat(draws, extent[axis_at] // parts).reshape([-1 if axis == axis_at else 1 for axis in range(len(extent))])
    return factor_of


def bell_draw(key, shape, spread, bound, pieces=(), kind=jnp.bfloat16):
    result = spread * jax.random.normal(key, shape, jnp.float32)
    if pieces:
        result = result * block_scale(key, shape, pieces, -0.22, 0.18)
    return jnp.clip(result, -bound, bound).astype(kind)


def setup_inputs(seed: int = 0, part: int = 0) -> dict:
    streams_of = jax.random.split(jax.random.key(seed), 8)
    part_keys = jax.random.split(jax.random.fold_in(streams_of[7], part), 8)
    backward_sensitivity = bell_draw(part_keys[0], (NWIN, 2, EPOCH_COUNT, EPOCH_COUNT), 4.0, 24.0, ((0, 16),))
    patch_stack_samples = draw_patch_stack_samples(jax.random.fold_in(jax.random.fold_in(streams_of[7], part), 71), part)
    patch_contribution_factor = jnp.clip(jnp.exp(math.log(2.0) - 2.3025851 * jax.random.uniform(part_keys[2], (NWIN, WIN), jnp.float32) ** block_scale(part_keys[2], (NWIN, WIN), ((0, 16),), -0.2, 0.2)), 0.2, 2.0)
    neighbour_displacements = draw_neighbour_displacements(jax.random.fold_in(jax.random.fold_in(streams_of[7], part), 71), part)
    delay_quanta = touch_ends(jax.random.randint(part_keys[4], (EPOCH_COUNT,), -16 * QUANT, 16 * QUANT), jax.random.fold_in(part_keys[4], 1), -16 * QUANT, (16 * QUANT) - 1).astype(jnp.int32)
    segment_correction_angles = jnp.clip(jax.random.uniform(part_keys[5], (EPOCH_COUNT, SEGMENT_COUNT), jnp.float32, -3.140625, 3.140625), -3.140625, 3.140625)
    segment_starts = draw_segment_starts(jax.random.fold_in(jax.random.fold_in(streams_of[7], part), 71), part)
    return {"backward_sensitivity": backward_sensitivity, "patch_stack_samples": patch_stack_samples, "patch_contribution_factor": patch_contribution_factor, "neighbour_displacements": neighbour_displacements, "delay_quanta": delay_quanta, "segment_correction_angles": segment_correction_angles, "segment_starts": segment_starts}


epsilon = 1e-06

def unit_angle(numerator, period):
    angle_value = 2.0 * jnp.pi / period * jnp.mod(numerator, period).astype(jnp.float32)
    return (jnp.cos(angle_value), jnp.sin(angle_value))

def product(left, right):
    return jnp.dot(left, right.T, preferred_element_type=jnp.float32)

def window_slots(operands):
    backward_sensitivity, patch_stack_samples, patch_contribution_factor = operands
    tap_total = jnp.sum(patch_contribution_factor)
    tapered = (patch_stack_samples * patch_contribution_factor[None, None, :]).astype(jnp.bfloat16)
    inverse_total = 1.0 / tap_total
    cov_real = (product(tapered[0], patch_stack_samples[0]) + product(tapered[1], patch_stack_samples[1])) * inverse_total
    cov_imag = (product(tapered[1], patch_stack_samples[0]) - product(tapered[0], patch_stack_samples[1])) * inverse_total
    power_sum = jnp.diagonal(cov_real) + epsilon
    amplitude = jnp.sqrt(power_sum)
    scaling = 1.0 / (amplitude[:, None] * amplitude[None, :])
    coh_real = cov_real * scaling
    coh_imag = cov_imag * scaling
    cot_real = backward_sensitivity[0].astype(jnp.float32)
    cot_imag = backward_sensitivity[1].astype(jnp.float32)
    correction = -lax.optimization_barrier(jnp.sum((cot_real + cot_real.T) * coh_real + (cot_imag - cot_imag.T) * coh_imag, axis=1)) / (2.0 * power_sum)
    adjusted_real = cot_real * scaling + jnp.diag(correction)
    adjusted_imag = cot_imag * scaling
    mixed_real = (adjusted_real + adjusted_real.T).astype(jnp.bfloat16)
    mixed_imag = (adjusted_imag - adjusted_imag.T).astype(jnp.bfloat16)
    grad_real = jnp.dot(mixed_real, patch_stack_samples[0], preferred_element_type=jnp.float32) - jnp.dot(mixed_imag, patch_stack_samples[1], preferred_element_type=jnp.float32)
    grad_imag = jnp.dot(mixed_imag, patch_stack_samples[0], preferred_element_type=jnp.float32) + jnp.dot(mixed_real, patch_stack_samples[1], preferred_element_type=jnp.float32)
    share = patch_contribution_factor / tap_total
    return (jnp.stack([grad_real, grad_imag]) * share[None, None, :]).astype(jnp.bfloat16)

def reference(backward_sensitivity, patch_stack_samples, patch_contribution_factor, neighbour_displacements, delay_quanta, segment_correction_angles, segment_starts):
    slot_grads = lax.map(window_slots, (backward_sensitivity, patch_stack_samples, patch_contribution_factor))
    tile_lines = WIN // RG
    hood_lines = NBHD // RG
    window_ids = jnp.arange(NWIN, dtype=jnp.int32)
    line_index = window_ids[:, None] * tile_lines - REACH + neighbour_displacements % hood_lines
    column_index = neighbour_displacements // hood_lines
    inside = (line_index >= 0) & (line_index < ALONG_TRACK_SIZE)
    target = jnp.where(inside, column_index * ALONG_TRACK_SIZE + line_index, RG * ALONG_TRACK_SIZE).reshape(-1)
    values = jnp.transpose(slot_grads, (1, 2, 0, 3)).reshape(2, EPOCH_COUNT, NWIN * WIN).astype(jnp.float32)
    sample_raster = jnp.zeros((2, EPOCH_COUNT, RG * ALONG_TRACK_SIZE + 1), jnp.float32).at[:, :, target].add(values)
    sample_raster = sample_raster[:, :, :RG * ALONG_TRACK_SIZE].reshape(2, EPOCH_COUNT, RG, ALONG_TRACK_SIZE)
    sample_positions = jnp.arange(ALONG_TRACK_SIZE, dtype=jnp.int32)
    segment_finder = lax.optimization_barrier(jnp.sum((sample_positions[None, :] >= segment_starts[:, None]).astype(jnp.int32), axis=0))
    along_track_rotor = segment_correction_angles[:, segment_finder]
    cosine = jnp.cos(along_track_rotor)[:, None, :]
    sine_line = jnp.sin(along_track_rotor)[:, None, :]
    input_real = cosine * sample_raster[0] + sine_line * sample_raster[1]
    input_imag = cosine * sample_raster[1] - sine_line * sample_raster[0]
    spectrum = jnp.fft.fft(input_real + 1j * input_imag, axis=-1)
    frequency = jnp.arange(ALONG_TRACK_SIZE, dtype=jnp.int32)
    signed = jnp.where(frequency < ALONG_TRACK_SIZE // 2, frequency, frequency - ALONG_TRACK_SIZE)
    filter_cos, filter_sin = unit_angle(signed[None, :] * delay_quanta[:, None], ALONG_TRACK_SIZE * QUANT)
    spectrum = spectrum * (filter_cos + 1j * filter_sin)[:, None, :]
    restored = jnp.fft.ifft(spectrum, axis=-1)
    return jnp.stack([restored.real, restored.imag]).astype(jnp.float32)
```

```python
import functools

import jax
import jax.numpy as jnp
import numpy as np
from jax import lax
from jax.experimental import pallas as pl
from jax.experimental.pallas import tpu as pltpu
from jax.sharding import PartitionSpec as P

EPOCHS = 256
LINES = 4096
RG = 8
WIN = 128
QUANT = 16
SEGMENTS = 9
MESH = pl.DeviceIdType.MESH
F32 = jnp.float32
BF16 = jnp.bfloat16


def windows_kernel(
    n, dates, wpd,
    g_hbm, z_hbm, wt_ref, disp_ref, x_hbm,
    gbuf, zbuf, lo_last, hi, pix, halo_out, halo_in, sendbuf,
    in_sem, halo_sem, send_sem, recv_sem, local_sem,
):
    me = lax.axis_index("date")
    chunks = wpd // 8

    def input_copies(w):
        return (
            pltpu.make_async_copy(g_hbm.at[w], gbuf.at[w], in_sem.at[w, 0]),
            pltpu.make_async_copy(z_hbm.at[w], zbuf.at[w], in_sem.at[w, 1]),
        )

    for w in [wpd - 1] + list(range(wpd - 1)):
        for copy in input_copies(w):
            copy.start()

    barrier = pltpu.get_barrier_semaphore()
    for k in range(1, n):
        pl.semaphore_signal(
            barrier, inc=1, device_id={"date": lax.rem(me + k, n)}, device_id_type=MESH
        )
    pl.semaphore_wait(barrier, n - 1)

    def window(w):
        for copy in input_copies(w):
            copy.wait()
        z0, z1 = zbuf[w, 0], zbuf[w, 1]
        z0f, z1f = z0.astype(F32), z1.astype(F32)
        wt = wt_ref[pl.ds(w, 1), :]
        inverse = 1.0 / jnp.sum(wt, axis=1, keepdims=True)
        q0 = (z0f * wt).astype(BF16).astype(F32)
        q1 = (z1f * wt).astype(BF16).astype(F32)
        power = jnp.sum(q0 * z0f + q1 * z1f, axis=1, keepdims=True) * inverse + 1e-6
        amp = lax.rsqrt(power)
        eye = lax.broadcasted_iota(jnp.int32, (EPOCHS, EPOCHS), 0) == lax.broadcasted_iota(
            jnp.int32, (EPOCHS, EPOCHS), 1
        )
        amp_row = jnp.sum(jnp.where(eye, amp, 0.0), axis=0, keepdims=True)
        scale = amp * amp_row
        g0, g1 = gbuf[w, 0], gbuf[w, 1]
        m0 = ((g0.astype(F32) + g0.T.astype(F32)) * scale).astype(BF16)
        m1 = ((g1.astype(F32) - g1.T.astype(F32)) * scale).astype(BF16)
        zcat = jnp.concatenate([z0, z1], axis=1)
        a0 = jnp.dot(m0, zcat, preferred_element_type=F32)
        a1 = jnp.dot(m1, zcat, preferred_element_type=F32)
        gre = a0[:, :WIN] - a1[:, WIN:]
        gim = a1[:, :WIN] + a0[:, WIN:]
        twice = -(jnp.sum(q0 * gre + q1 * gim, axis=1, keepdims=True) * inverse) / power
        share = wt * inverse
        s0 = ((gre + twice * z0f) * share).astype(BF16)
        s1 = ((gim + twice * z1f) * share).astype(BF16)
        seat = lax.broadcasted_iota(jnp.int32, (2 * WIN, WIN), 0)
        near = (seat >= WIN).astype(jnp.int32)
        inner = seat - near * WIN
        line = inner % 16 + 16 * near
        label = (inner // 16) * 32 + line
        first = jnp.logical_and(me == 0, w == 0).astype(jnp.int32)
        final = jnp.logical_and(me == n - 1, w == wpd - 1).astype(jnp.int32)
        off = (line < 8).astype(jnp.int32) * first + (line >= 24).astype(jnp.int32) * final
        label = label - off * 4096
        chooser = (label == disp_ref[pl.ds(w, 1), :]).astype(F32).astype(BF16)
        dims = (((1,), (1,)), ((), ()))
        return (
            lax.dot_general(s0, chooser, dims, preferred_element_type=F32),
            lax.dot_general(s1, chooser, dims, preferred_element_type=F32),
        )

    spread = window(wpd - 1)
    for c in range(2):
        lo_last[pl.ds(c * EPOCHS, EPOCHS), :] = spread[c][:, :WIN]
        halo_out[pl.ds(c * EPOCHS, EPOCHS), :] = spread[c][:, WIN:].astype(BF16)
    halo = pltpu.make_async_remote_copy(
        src_ref=halo_out, dst_ref=halo_in, send_sem=halo_sem.at[0], recv_sem=halo_sem.at[1],
        device_id={"date": lax.rem(me + 1, n)}, device_id_type=MESH,
    )
    halo.start()
    hi[...] = jnp.zeros_like(hi)

    lane = lax.broadcasted_iota(jnp.int32, (2 * dates, WIN), 1)

    def send_copy(g, k):
        e = lax.rem(me + k, n)
        return pltpu.make_async_remote_copy(
            src_ref=sendbuf.at[g, e], dst_ref=x_hbm.at[g, me],
            send_sem=send_sem.at[g, k], recv_sem=recv_sem.at[g, k],
            device_id={"date": e}, device_id_type=MESH,
        )

    for g in range(chunks):
        count = 8 if g < chunks - 1 else 7

        def step(b, carry):
            spread = window(b + 8 * g)
            for c in range(2):
                rows = pl.ds(c * EPOCHS, EPOCHS)
                pix[b, rows, :] = spread[c][:, :WIN] + hi[rows, :]
                hi[rows, :] = spread[c][:, WIN:]
            return carry

        lax.fori_loop(0, count, step, 0)
        if g == 0:
            halo.wait()
            pix[0] = pix[0] + halo_in[...].astype(F32)
        if g == chunks - 1:
            pix[7] = lo_last[...] + hi[...]

        def relayout(e):
            items = []
            for b in range(8):
                items.append(jnp.concatenate([
                    pix[b, pl.ds(pl.multiple_of(e * dates, 8), dates), :],
                    pix[b, pl.ds(pl.multiple_of(EPOCHS + e * dates, 8), dates), :],
                ], axis=0))
            for bit in (4, 2, 1):
                keep = (lane // (16 * bit)) % 2 == 0
                for b in range(8):
                    if b & bit == 0:
                        low, high = items[b], items[b + bit]
                        items[b] = jnp.where(keep, low, pltpu.roll(high, 16 * bit, 1))
                        items[b + bit] = jnp.where(keep, pltpu.roll(low, WIN - 16 * bit, 1), high)
            for column in range(8):
                sendbuf[g, e, column] = items[column].astype(BF16)

        def send(k, carry):
            relayout(lax.rem(me + k, n))
            send_copy(g, k).start()
            return carry

        lax.fori_loop(1, n, send, 0)
        relayout(me)
        pltpu.make_async_copy(sendbuf.at[g, me], x_hbm.at[g, me], local_sem.at[g]).start()

    for g in range(chunks):
        pltpu.make_async_copy(sendbuf.at[g, me], x_hbm.at[g, me], local_sem.at[g]).wait()

        def drain(k, carry):
            send_copy(g, k).wait()
            return carry

        lax.fori_loop(1, n, drain, 0)


def windows_call(n, g, z, wt, disp):
    wpd = g.shape[0]
    dates = EPOCHS // n
    chunks = wpd // 8
    return pl.pallas_call(
        functools.partial(windows_kernel, n, dates, wpd),
        out_shape=jax.ShapeDtypeStruct((chunks, n, RG, 2 * dates, WIN), BF16),
        in_specs=[pl.BlockSpec(memory_space=pl.ANY)] * 2
        + [pl.BlockSpec(memory_space=pltpu.VMEM)] * 2,
        out_specs=pl.BlockSpec(memory_space=pl.ANY),
        scratch_shapes=[
            pltpu.VMEM((wpd, 2, EPOCHS, EPOCHS), BF16),
            pltpu.VMEM((wpd, 2, EPOCHS, WIN), BF16),
            pltpu.VMEM((2 * EPOCHS, WIN), F32),
            pltpu.VMEM((2 * EPOCHS, WIN), F32),
            pltpu.VMEM((8, 2 * EPOCHS, WIN), F32),
            pltpu.VMEM((2 * EPOCHS, WIN), BF16),
            pltpu.VMEM((2 * EPOCHS, WIN), BF16),
            pltpu.VMEM((chunks, n, RG, 2 * dates, WIN), BF16),
            pltpu.SemaphoreType.DMA((wpd, 2)),
            pltpu.SemaphoreType.DMA((2,)),
            pltpu.SemaphoreType.DMA((chunks, n)),
            pltpu.SemaphoreType.DMA((chunks, n)),
            pltpu.SemaphoreType.DMA((chunks,)),
        ],
        compiler_params=pltpu.CompilerParams(
            collective_id=0, has_side_effects=True, vmem_limit_bytes=40 * 1024 * 1024
        ),
        name="windows",
    )(g, z, wt, disp)


def butterfly(real, imag, sign):
    n = len(real)
    if n == 1:
        return real, imag
    er, ei = butterfly(real[0::2], imag[0::2], sign)
    our, oui = butterfly(real[1::2], imag[1::2], sign)
    half = n // 2
    out_r, out_i = [None] * n, [None] * n
    for k in range(half):
        xr, xi = our[k], oui[k]
        if k == 0:
            tr, ti = xr, xi
        elif 4 * k == n:
            tr, ti = (xi, -xr) if sign < 0 else (-xi, xr)
        else:
            angle = sign * 2.0 * np.pi * k / n
            c, s = float(np.cos(angle)), float(np.sin(angle))
            tr, ti = xr * c - xi * s, xr * s + xi * c
        out_r[k], out_i[k] = er[k] + tr, ei[k] + ti
        out_r[k + half], out_i[k + half] = er[k] - tr, ei[k] - ti
    return out_r, out_i


def split(value):
    high = value.astype(BF16)
    return high, (value - high.astype(F32)).astype(BF16)


def filter_kernel(
    n, dates, reach,
    starts_ref, x_ref, delay_ref, angle_ref, mats_ref, tw_ref, o_hbm,
    phase, twist, xp, yh, yl, u, out, out_sem,
):
    chunks = reach // WIN
    unit = float(2.0 * np.pi / (LINES * QUANT))
    period = LINES * QUANT
    delay = delay_ref[...] + 8 * QUANT
    cosines, sines = jnp.cos(angle_ref[...]), jnp.sin(angle_ref[...])
    for s in range(n):
        position = s * reach + lax.broadcasted_iota(jnp.int32, (dates, reach), 1) - 8
        position = jnp.where(position < 0, position + LINES, position)
        pc = jnp.broadcast_to(cosines[:, 0:1], (dates, reach))
        ps = jnp.broadcast_to(sines[:, 0:1], (dates, reach))
        for j in range(1, SEGMENTS):
            later = position >= starts_ref[j - 1]
            pc = jnp.where(later, cosines[:, j : j + 1], pc)
            ps = jnp.where(later, sines[:, j : j + 1], ps)
        phase[0, s], phase[1, s] = pc, ps
    rows = (lax.broadcasted_iota(jnp.int32, (dates, WIN), 1) * delay) & (period - 1)
    row_angle = rows.astype(F32) * unit
    row_c, row_s = jnp.cos(row_angle), jnp.sin(row_angle)
    for k in range(n):
        bc, bs = tw_ref[0, k : k + 1, :], tw_ref[1, k : k + 1, :]
        rc, rs = row_c[:, k : k + 1], row_s[:, k : k + 1]
        twist[0, k] = rc * bc + rs * bs
        twist[1, k] = rs * bc - rc * bs
    lanes = lax.broadcasted_iota(jnp.int32, (dates, reach), 1)
    lanes = jnp.where(lanes < reach // 2, lanes, lanes - reach) * n
    lane_angle = ((lanes * delay) & (period - 1)).astype(F32) * unit
    lane_c = jnp.concatenate([jnp.cos(lane_angle)] * n, axis=0)
    lane_s = jnp.concatenate([jnp.sin(lane_angle)] * n, axis=0)

    def product(which):
        high, low = yh[...], yl[...]
        mh, ml = mats_ref[which, 0], mats_ref[which, 1]
        return (
            jnp.dot(high, mh, preferred_element_type=F32)
            + jnp.dot(low, mh, preferred_element_type=F32)
            + jnp.dot(high, ml, preferred_element_type=F32)
        )

    def column(col, carry):
        for lt in range(chunks):
            lane = pl.ds(lt * WIN, WIN)
            for s in range(n):
                x = x_ref[lt, s, col].astype(F32)
                xr, xi = x[:dates], x[dates:]
                pc, ps = phase[0, s, :, lane], phase[1, s, :, lane]
                xp[0, s] = pc * xr + ps * xi
                xp[1, s] = pc * xi - ps * xr
            for dh in range(dates // 8):
                row = pl.ds(dh * 8, 8)
                yr, yi = butterfly(
                    [xp[0, s, row, :] for s in range(n)], [xp[1, s, row, :] for s in range(n)], -1
                )
                for k in range(n):
                    tc, ts = twist[0, k, row, lane], twist[1, k, row, lane]
                    u[pl.ds(k * dates + dh * 8, 8), lane] = yr[k] * tc - yi[k] * ts
                    u[pl.ds(k * dates + dh * 8, 8), pl.ds(reach + lt * WIN, WIN)] = (
                        yr[k] * ts + yi[k] * tc
                    )
        yh[...], yl[...] = split(u[...])
        spec = product(0)
        sr, si = spec[:, :reach], spec[:, reach:]
        rh, rl = split(sr * lane_c - si * lane_s)
        ih, il = split(sr * lane_s + si * lane_c)
        yh[:, :reach], yh[:, reach:] = rh, ih
        yl[:, :reach], yl[:, reach:] = rl, il
        u[...] = product(1)
        for lt in range(chunks):
            lane = pl.ds(lt * WIN, WIN)
            for dh in range(dates // 8):
                vr, vi = [], []
                for k in range(n):
                    ur = u[pl.ds(k * dates + dh * 8, 8), lane]
                    ui = u[pl.ds(k * dates + dh * 8, 8), pl.ds(reach + lt * WIN, WIN)]
                    bc, bs = tw_ref[0, k : k + 1, lane], tw_ref[1, k : k + 1, lane]
                    vr.append(ur * bc - ui * bs)
                    vi.append(ur * bs + ui * bc)
                vr, vi = butterfly(vr, vi, 1)
                for h in range(n):
                    for c, v in ((0, vr[h]), (1, vi[h])):
                        out[h * chunks + lt, pl.ds((c * dates + dh * 8) * RG + col, 8, stride=RG), :] = v
        return carry

    lax.fori_loop(0, RG, column, 0)
    copies = [
        pltpu.make_async_copy(out.at[t], o_hbm.at[:, pl.ds(t * WIN, WIN)], out_sem.at[t])
        for t in range(LINES // WIN)
    ]
    for copy in copies:
        copy.start()
    for copy in copies:
        copy.wait()


def filter_call(n, x, delay, angles, starts):
    dates = delay.shape[0]
    reach = LINES // n
    grid = np.outer(np.arange(reach), np.arange(reach)) % reach * (2.0 * np.pi / reach)
    c, s = np.cos(grid), np.sin(grid)
    forward = np.block([[c, -s], [s, c]])
    inverse = np.block([[c, s], [-s, c]]) / LINES
    mats = []
    for m in (forward, inverse):
        high = m.astype(jnp.bfloat16)
        low = (m - high.astype(np.float64)).astype(jnp.bfloat16)
        mats.append(np.stack([high, low]))
    mats = np.stack(mats)
    base = np.outer(np.arange(n), np.arange(reach)) * (2.0 * np.pi / LINES)
    twiddle = np.stack([np.cos(base), np.sin(base)]).astype(np.float32)
    vmem = pl.BlockSpec(memory_space=pltpu.VMEM)
    out = pl.pallas_call(
        functools.partial(filter_kernel, n, dates, reach),
        out_shape=jax.ShapeDtypeStruct((2 * dates * RG, LINES), F32),
        in_specs=[pl.BlockSpec(memory_space=pltpu.SMEM)] + [vmem] * 5,
        out_specs=pl.BlockSpec(memory_space=pl.ANY),
        scratch_shapes=[
            pltpu.VMEM((2, n, dates, reach), F32),
            pltpu.VMEM((2, n, dates, reach), F32),
            pltpu.VMEM((2, n, dates, WIN), F32),
            pltpu.VMEM((n * dates, 2 * reach), BF16),
            pltpu.VMEM((n * dates, 2 * reach), BF16),
            pltpu.VMEM((n * dates, 2 * reach), F32),
            pltpu.VMEM((LINES // WIN, 2 * dates * RG, WIN), F32),
            pltpu.SemaphoreType.DMA((LINES // WIN,)),
        ],
        compiler_params=pltpu.CompilerParams(vmem_limit_bytes=40 * 1024 * 1024),
        name="shift_filter",
    )(starts, x, delay[:, None], angles, jnp.asarray(mats), jnp.asarray(twiddle))
    return out.reshape(2, dates, RG, LINES)


def solution(mesh):
    n = mesh.shape["date"]

    def on_device(g, z, wt, disp, delay, angles, starts):
        x = windows_call(n, g, z, wt, disp)
        return filter_call(n, x, delay, angles, starts)

    both = ("frames", "date")
    return jax.shard_map(
        on_device,
        mesh=mesh,
        in_specs=(
            P(both, None, None, None),
            P(both, None, None, None),
            P(both, None),
            P(both, None),
            P(both),
            P(both, None),
            P("frames"),
        ),
        out_specs=P(None, both, None, None),
        check_vma=False,
    )
```

```python
import functools

import jax
import jax.numpy as jnp
import numpy as np
from jax import lax
from jax.experimental import pallas as pl
from jax.experimental.pallas import tpu as pltpu
from jax.sharding import PartitionSpec as P

EPOCHS = 256
LINES = 4096
RG = 8
WIN = 128
QUANT = 16
SEGMENTS = 9
PIECE = 2
MESH = pl.DeviceIdType.MESH
F32 = jnp.float32
BF16 = jnp.bfloat16


def butterfly(real, imag, sign):
    n = len(real)
    if n == 1:
        return real, imag
    er, ei = butterfly(real[0::2], imag[0::2], sign)
    our, oui = butterfly(real[1::2], imag[1::2], sign)
    half = n // 2
    out_r, out_i = [None] * n, [None] * n
    for k in range(half):
        xr, xi = our[k], oui[k]
        if k == 0:
            tr, ti = xr, xi
        elif 4 * k == n:
            tr, ti = (xi, -xr) if sign < 0 else (-xi, xr)
        else:
            angle = sign * 2.0 * np.pi * k / n
            c, s = float(np.cos(angle)), float(np.sin(angle))
            tr, ti = xr * c - xi * s, xr * s + xi * c
        out_r[k], out_i[k] = er[k] + tr, ei[k] + ti
        out_r[k + half], out_i[k + half] = er[k] - tr, ei[k] - ti
    return out_r, out_i


def split(value):
    high = value.astype(BF16)
    return high, (value - high.astype(F32)).astype(BF16)


def kernel(
    n, dates, wpd,
    starts_ref, delay_ref, g_hbm, z_hbm, wt_hbm, disp_hbm, angle_hbm, out,
    gbuf, zbuf, wt_ref, disp_ref, angle_ref, mats_ref, tw_ref,
    lo_last, hi, pix, halo_out, halo_in, sendbuf, x_ref,
    phase, twist, rotor, yh, yl, xp, u,
    in_sem, table_sem, halo_sem, send_sem, recv_sem,
):
    me = lax.axis_index("date")
    chunks = wpd // 8

    def input_copies(w):
        return (
            pltpu.make_async_copy(g_hbm.at[w], gbuf.at[w], in_sem.at[w, 0]),
            pltpu.make_async_copy(z_hbm.at[w], zbuf.at[w], in_sem.at[w, 1]),
        )

    table_copies = [
        pltpu.make_async_copy(source, target, table_sem.at[i])
        for i, (source, target) in enumerate((
            (wt_hbm, wt_ref), (disp_hbm, disp_ref), (angle_hbm, angle_ref),
        ))
    ]
    for copy in table_copies[:2]:
        copy.start()
    for w in [wpd - 1] + list(range(wpd - 1)):
        for copy in input_copies(w):
            copy.start()
    for copy in table_copies[2:]:
        copy.start()

    barrier = pltpu.get_barrier_semaphore()
    for k in range(1, n):
        pl.semaphore_signal(
            barrier, inc=1, device_id={"date": lax.rem(me + k, n)}, device_id_type=MESH
        )
    pl.semaphore_wait(barrier, n - 1)

    def window(w):
        for copy in input_copies(w):
            copy.wait()
        z0, z1 = zbuf[w, 0], zbuf[w, 1]
        z0f, z1f = z0.astype(F32), z1.astype(F32)
        wt = wt_ref[pl.ds(w, 1), :]
        inverse = 1.0 / jnp.sum(wt, axis=1, keepdims=True)
        q0 = (z0f * wt).astype(BF16).astype(F32)
        q1 = (z1f * wt).astype(BF16).astype(F32)
        power = jnp.sum(q0 * z0f + q1 * z1f, axis=1, keepdims=True) * inverse + 1e-6
        amp = lax.rsqrt(power)
        eye = lax.broadcasted_iota(jnp.int32, (EPOCHS, EPOCHS), 0) == lax.broadcasted_iota(
            jnp.int32, (EPOCHS, EPOCHS), 1
        )
        amp_row = jnp.sum(jnp.where(eye, amp, 0.0), axis=0, keepdims=True)
        scale = amp * amp_row
        g0, g1 = gbuf[w, 0], gbuf[w, 1]
        m0 = ((g0.astype(F32) + g0.T.astype(F32)) * scale).astype(BF16)
        m1 = ((g1.astype(F32) - g1.T.astype(F32)) * scale).astype(BF16)
        zcat = jnp.concatenate([z0, z1], axis=1)
        a0 = jnp.dot(m0, zcat, preferred_element_type=F32)
        a1 = jnp.dot(m1, zcat, preferred_element_type=F32)
        gre = a0[:, :WIN] - a1[:, WIN:]
        gim = a1[:, :WIN] + a0[:, WIN:]
        twice = -(jnp.sum(q0 * gre + q1 * gim, axis=1, keepdims=True) * inverse) / power
        share = wt * inverse
        s0 = ((gre + twice * z0f) * share).astype(BF16)
        s1 = ((gim + twice * z1f) * share).astype(BF16)
        seat = lax.broadcasted_iota(jnp.int32, (2 * WIN, WIN), 0)
        near = (seat >= WIN).astype(jnp.int32)
        inner = seat - near * WIN
        line = inner % 16 + 16 * near
        label = (inner // 16) * 32 + line
        first = jnp.logical_and(me == 0, w == 0).astype(jnp.int32)
        final = jnp.logical_and(me == n - 1, w == wpd - 1).astype(jnp.int32)
        off = (line < 8).astype(jnp.int32) * first + (line >= 24).astype(jnp.int32) * final
        label = label - off * 4096
        chooser = (label == disp_ref[pl.ds(w, 1), :]).astype(F32).astype(BF16)
        dims = (((1,), (1,)), ((), ()))
        return (
            lax.dot_general(s0, chooser, dims, preferred_element_type=F32),
            lax.dot_general(s1, chooser, dims, preferred_element_type=F32),
        )

    for copy in table_copies[:2]:
        copy.wait()
    spread = window(wpd - 1)
    for c in range(2):
        lo_last[pl.ds(c * EPOCHS, EPOCHS), :] = spread[c][:, :WIN]
        halo_out[pl.ds(c * EPOCHS, EPOCHS), :] = spread[c][:, WIN:].astype(BF16)
    halo = pltpu.make_async_remote_copy(
        src_ref=halo_out, dst_ref=halo_in, send_sem=halo_sem.at[0], recv_sem=halo_sem.at[1],
        device_id={"date": lax.rem(me + 1, n)}, device_id_type=MESH,
    )
    halo.start()
    hi[...] = jnp.zeros_like(hi)

    lane = lax.broadcasted_iota(jnp.int32, (2 * dates, WIN), 1)

    pieces = RG // PIECE

    def partner(j):
        return n // 2 + (2 * (j % 2) - 1) * (j // 2)

    def chunk_copy(g, k):
        e = lax.rem(me + k, n)
        return pltpu.make_async_remote_copy(
            src_ref=sendbuf.at[g, e], dst_ref=x_ref.at[g, me],
            send_sem=send_sem.at[g, k], recv_sem=recv_sem.at[g, k],
            device_id={"date": e}, device_id_type=MESH,
        )

    def piece_copy(p, k):
        e = lax.rem(me + k, n)
        columns = pl.ds(p * PIECE, PIECE)
        return pltpu.make_async_remote_copy(
            src_ref=sendbuf.at[chunks - 1, e, columns], dst_ref=x_ref.at[chunks - 1, me, columns],
            send_sem=send_sem.at[chunks - 1 + p, k], recv_sem=recv_sem.at[chunks - 1 + p, k],
            device_id={"date": e}, device_id_type=MESH,
        )

    for g in range(chunks):
        count = 8 if g < chunks - 1 else 7

        def step(b, carry):
            spread = window(b + 8 * g)
            for c in range(2):
                rows = pl.ds(c * EPOCHS, EPOCHS)
                pix[b, rows, :] = spread[c][:, :WIN] + hi[rows, :]
                hi[rows, :] = spread[c][:, WIN:]
            return carry

        lax.fori_loop(0, count, step, 0)
        if g == 0:
            halo.wait()
            pix[0] = pix[0] + halo_in[...].astype(F32)
        if g == chunks - 1:
            pix[7] = lo_last[...] + hi[...]

        def relayout(e, target):
            items = []
            for b in range(8):
                items.append(jnp.concatenate([
                    pix[b, pl.ds(pl.multiple_of(e * dates, 8), dates), :],
                    pix[b, pl.ds(pl.multiple_of(EPOCHS + e * dates, 8), dates), :],
                ], axis=0))
            for bit in (4, 2, 1):
                keep = (lane // (16 * bit)) % 2 == 0
                for b in range(8):
                    if b & bit == 0:
                        low, high = items[b], items[b + bit]
                        items[b] = jnp.where(keep, low, pltpu.roll(high, 16 * bit, 1))
                        items[b + bit] = jnp.where(keep, pltpu.roll(low, WIN - 16 * bit, 1), high)
            for column in range(8):
                target[g, e, column] = items[column].astype(BF16)

        def send(j, carry):
            k = partner(j)
            relayout(lax.rem(me + k, n), sendbuf)
            if g < chunks - 1:
                chunk_copy(g, k).start()
            else:
                piece_copy(0, k).start()
            return carry

        lax.fori_loop(1, n, send, 0)
        relayout(me, x_ref)

    def send_pieces(i, carry):
        piece_copy(1 + i // (n - 1), partner(1 + i % (n - 1))).start()
        return carry

    lax.fori_loop(0, (pieces - 1) * (n - 1), send_pieces, 0)
    for copy in table_copies[2:]:
        copy.wait()
    reach = LINES // n
    unit = float(2.0 * np.pi / (LINES * QUANT))
    period = LINES * QUANT
    index = lax.broadcasted_iota(jnp.int32, (dates, 1), 0)
    delay = jnp.full((dates, 1), 8 * QUANT, jnp.int32)
    for d in range(dates):
        delay = delay + jnp.where(index == d, delay_ref[d], 0)
    grid = lax.broadcasted_iota(jnp.int32, (reach, reach), 0) * lax.broadcasted_iota(
        jnp.int32, (reach, reach), 1
    )
    grid = (grid & (reach - 1)).astype(F32) * float(2.0 * np.pi / reach)
    grid_c, grid_s = jnp.cos(grid), jnp.sin(grid)
    for which, (a, b, c, d) in enumerate((
        (grid_c, -grid_s, grid_s, grid_c),
        (grid_c * (1.0 / LINES), grid_s * (1.0 / LINES), grid_s * (-1.0 / LINES), grid_c * (1.0 / LINES)),
    )):
        for i, block in enumerate((a, b, c, d)):
            rows, lanes = pl.ds(i // 2 * reach, reach), pl.ds(i % 2 * reach, reach)
            mats_ref[which, 0, rows, lanes], mats_ref[which, 1, rows, lanes] = split(block)
    base = lax.broadcasted_iota(jnp.int32, (n, reach), 0) * lax.broadcasted_iota(
        jnp.int32, (n, reach), 1
    )
    base = base.astype(F32) * float(2.0 * np.pi / LINES)
    tw_ref[0], tw_ref[1] = jnp.cos(base), jnp.sin(base)
    cosines, sines = jnp.cos(angle_ref[...]), jnp.sin(angle_ref[...])
    for s in range(n):
        position = s * reach + lax.broadcasted_iota(jnp.int32, (dates, reach), 1) - 8
        position = jnp.where(position < 0, position + LINES, position)
        pc = jnp.broadcast_to(cosines[:, 0:1], (dates, reach))
        ps = jnp.broadcast_to(sines[:, 0:1], (dates, reach))
        for j in range(1, SEGMENTS):
            later = position >= starts_ref[j - 1]
            pc = jnp.where(later, cosines[:, j : j + 1], pc)
            ps = jnp.where(later, sines[:, j : j + 1], ps)
        phase[0, s], phase[1, s] = pc, ps
    rows = (lax.broadcasted_iota(jnp.int32, (dates, WIN), 1) * delay) & (period - 1)
    row_angle = rows.astype(F32) * unit
    row_c, row_s = jnp.cos(row_angle), jnp.sin(row_angle)
    for k in range(n):
        bc, bs = tw_ref[0, k : k + 1, :], tw_ref[1, k : k + 1, :]
        rc, rs = row_c[:, k : k + 1], row_s[:, k : k + 1]
        twist[0, k] = rc * bc + rs * bs
        twist[1, k] = rs * bc - rc * bs
    lanes = lax.broadcasted_iota(jnp.int32, (dates, reach), 1)
    lanes = jnp.where(lanes < reach // 2, lanes, lanes - reach) * n
    lane_angle = ((lanes * delay) & (period - 1)).astype(F32) * unit
    rotor[0] = jnp.concatenate([jnp.cos(lane_angle)] * n, axis=0)
    rotor[1] = jnp.concatenate([jnp.sin(lane_angle)] * n, axis=0)

    def product(which):
        high, low = yh[...], yl[...]
        mh, ml = mats_ref[which, 0], mats_ref[which, 1]
        return (
            jnp.dot(high, mh, preferred_element_type=F32)
            + jnp.dot(low, mh, preferred_element_type=F32)
            + jnp.dot(high, ml, preferred_element_type=F32)
        )

    def column(col, carry):
        for lt in range(chunks):
            lane = pl.ds(lt * WIN, WIN)
            for s in range(n):
                x = x_ref[lt, s, col].astype(F32)
                xr, xi = x[:dates], x[dates:]
                pc, ps = phase[0, s, :, lane], phase[1, s, :, lane]
                xp[0, s] = pc * xr + ps * xi
                xp[1, s] = pc * xi - ps * xr
            for dh in range(dates // 8):
                row = pl.ds(dh * 8, 8)
                yr, yi = butterfly(
                    [xp[0, s, row, :] for s in range(n)], [xp[1, s, row, :] for s in range(n)], -1
                )
                for k in range(n):
                    tc, ts = twist[0, k, row, lane], twist[1, k, row, lane]
                    u[pl.ds(k * dates + dh * 8, 8), lane] = yr[k] * tc - yi[k] * ts
                    u[pl.ds(k * dates + dh * 8, 8), pl.ds(reach + lt * WIN, WIN)] = (
                        yr[k] * ts + yi[k] * tc
                    )
        yh[...], yl[...] = split(u[...])
        spec = product(0)
        lane_c, lane_s = rotor[0], rotor[1]
        sr, si = spec[:, :reach], spec[:, reach:]
        rh, rl = split(sr * lane_c - si * lane_s)
        ih, il = split(sr * lane_s + si * lane_c)
        yh[:, :reach], yh[:, reach:] = rh, ih
        yl[:, :reach], yl[:, reach:] = rl, il
        u[...] = product(1)
        for lt in range(chunks):
            lane = pl.ds(lt * WIN, WIN)
            for dh in range(dates // 8):
                vr, vi = [], []
                for k in range(n):
                    ur = u[pl.ds(k * dates + dh * 8, 8), lane]
                    ui = u[pl.ds(k * dates + dh * 8, 8), pl.ds(reach + lt * WIN, WIN)]
                    bc, bs = tw_ref[0, k : k + 1, lane], tw_ref[1, k : k + 1, lane]
                    vr.append(ur * bc - ui * bs)
                    vi.append(ur * bs + ui * bc)
                vr, vi = butterfly(vr, vi, 1)
                for h in range(n):
                    for c, v in ((0, vr[h]), (1, vi[h])):
                        tile = (c * dates + dh * 8) * (LINES // WIN) + h * chunks + lt
                        out[pl.ds(tile * RG + col, 8, stride=RG * (LINES // WIN)), :] = v
        return carry

    for g in range(chunks - 1):

        def drain(k, carry):
            chunk_copy(g, k).wait()
            return carry

        lax.fori_loop(1, n, drain, 0)

    def piece(p, carry):
        def drain(k, carry):
            piece_copy(p, k).wait()
            return carry

        lax.fori_loop(1, n, drain, 0)
        lax.fori_loop(p * PIECE, (p + 1) * PIECE, column, 0)
        return carry

    lax.fori_loop(0, pieces, piece, 0)


def call(n, g, z, wt, disp, delay, angles, starts):
    wpd = g.shape[0]
    chunks = wpd // 8
    dates = EPOCHS // n
    reach = LINES // n
    smem = pl.BlockSpec(memory_space=pltpu.SMEM)
    hbm = pl.BlockSpec(memory_space=pl.ANY)
    messages = chunks - 1 + RG // PIECE
    out = pl.pallas_call(
        functools.partial(kernel, n, dates, wpd),
        out_shape=jax.ShapeDtypeStruct((2 * dates * RG * (LINES // WIN), WIN), F32),
        in_specs=[smem] * 2 + [hbm] * 5,
        out_specs=pl.BlockSpec(memory_space=pltpu.VMEM),
        scratch_shapes=[
            pltpu.VMEM((wpd, 2, EPOCHS, EPOCHS), BF16),
            pltpu.VMEM((wpd, 2, EPOCHS, WIN), BF16),
            pltpu.VMEM((wpd, WIN), F32),
            pltpu.VMEM((wpd, WIN), jnp.int32),
            pltpu.VMEM((dates, SEGMENTS), F32),
            pltpu.VMEM((2, 2, 2 * reach, 2 * reach), BF16),
            pltpu.VMEM((2, n, reach), F32),
            pltpu.VMEM((2 * EPOCHS, WIN), F32),
            pltpu.VMEM((2 * EPOCHS, WIN), F32),
            pltpu.VMEM((8, 2 * EPOCHS, WIN), F32),
            pltpu.VMEM((2 * EPOCHS, WIN), BF16),
            pltpu.VMEM((2 * EPOCHS, WIN), BF16),
            pltpu.VMEM((chunks, n, RG, 2 * dates, WIN), BF16),
            pltpu.VMEM((chunks, n, RG, 2 * dates, WIN), BF16),
            pltpu.VMEM((2, n, dates, reach), F32),
            pltpu.VMEM((2, n, dates, reach), F32),
            pltpu.VMEM((2, n * dates, reach), F32),
            pltpu.VMEM((n * dates, 2 * reach), BF16),
            pltpu.VMEM((n * dates, 2 * reach), BF16),
            pltpu.VMEM((2, n, dates, WIN), F32),
            pltpu.VMEM((n * dates, 2 * reach), F32),
            pltpu.SemaphoreType.DMA((wpd, 2)),
            pltpu.SemaphoreType.DMA((3,)),
            pltpu.SemaphoreType.DMA((2,)),
            pltpu.SemaphoreType.DMA((messages, n)),
            pltpu.SemaphoreType.DMA((messages, n)),
        ],
        compiler_params=pltpu.CompilerParams(
            collective_id=0, has_side_effects=True, vmem_limit_bytes=60 * 1024 * 1024
        ),
        name="adjoint",
    )(starts, delay, g, z, wt, disp, angles)
    out = out.reshape(2, dates, LINES // WIN, RG, WIN)
    return jnp.transpose(out, (0, 1, 3, 2, 4)).reshape(2, dates, RG, LINES)


def solution(mesh):
    n = mesh.shape["date"]

    def on_device(g, z, wt, disp, delay, angles, starts):
        return call(n, g, z, wt, disp, delay, angles, starts)

    both = ("frames", "date")
    return jax.shard_map(
        on_device,
        mesh=mesh,
        in_specs=(
            P(both, None, None, None),
            P(both, None, None, None),
            P(both, None),
            P(both, None),
            P(both),
            P(both, None),
            P("frames"),
        ),
        out_specs=P(None, both, None, None),
        check_vma=False,
    )
```
